32 devices in a mesh: dp: 4 (over y, core), tensor: 8 (over z, x).
Axes of the slice: x: 2, y: 2, z: 4, core: 2. Of those that a mesh axis runs over, the one named last changes fastest.
Arguments:
- attn_in: bfloat16 [512, 2048], P('dp', 'tensor'), parts along dimension 0, may hold values from -127 to 127
- wo_int: bfloat16 [2048, 8192], P('tensor'), may hold values from -127 to 127
- wo_exponent: int32 [8192], replicated, may hold values from -15 to -12
- token_scale: float32 [512], P(('dp', 'tensor')), parts along dimension 0, may hold values from 0.3 to 3
- residual: bfloat16 [512, 8192], P(('dp', 'tensor')), parts along dimension 0, may hold values from -6 to 6
- norm_gain: float32 [8192], replicated, may hold values from 0.5 to 1.5
- gate_int: bfloat16 [8192, 2048], P(None, 'tensor'), may hold values from -127 to 127, as said below
- up_int: bfloat16 [8192, 2048], P(None, 'tensor'), may hold values from -127 to 127, as said below
- gate_exponent: int32 [2048], P('tensor'), may hold values from -14 to -12
- up_exponent: int32 [2048], P('tensor'), may hold values from -14 to -12
Outputs:
- hidden: bfloat16 [512, 2048], P('dp', 'tensor'), parts along dimension 0
- checksum: float32 [32, 8192], P(('dp', 'tensor')), parts along dimension 0
The draws below stay inside these ranges and needn't reach their ends.
There are 4 independent parts, one for each index of `dp`. The reference program is written for one: setup_inputs(seed, part) draws one part's arguments, and reference() takes and returns one part's arrays. A program takes and returns all parts, laid end to end along the dimension named above; an argument that names none is the same for every part. Nothing has to cross between parts.
Inputs may be any that keep to these rules, and one draw needn't show every extreme that they name: `gate_int`: integer values. `up_int`: integer values.
All inputs are finite; a program needn't handle non-finite values.
Results may differ from the reference program's by a relative error of at most 0.035.
Values may be sent and summed in bfloat16 or wider, within the bound.
A program may use at most 64 MiB of HBM per device.

```python
import math
import jax
import jax.numpy as jnp
from jax import lax

D = 8192
D_LOG = 13
TOK_DEV = 16
TOKENS = 128
HW = 2048
FF_WIN = 2048
N_TENSOR = 8


def int_table(key, shape):
    return jax.random.randint(key, shape, -127, 128).astype(jnp.float32).astype(jnp.bfloat16)


def draw_attn_in(key, part):
    first, second, third, fourth = jax.random.split(jax.random.fold_in(key, 3), 4)
    half_width = HW // 2
    amplitude = jax.random.randint(first, (TOKENS, 1), 32, 128)
    nudges = jax.random.randint(third, (TOKENS, half_width), -2, 3)
    raw_bits = jax.random.randint(second, (TOKENS, half_width), 0, 65536)
    values = raw_bits * (2 * amplitude + 1) // 65536 - amplitude
    partner = jnp.clip(values + nudges, -127, 127)
    joined = jnp.concatenate([values, partner], axis=1).astype(jnp.float32)
    jitter = jax.random.uniform(fourth, (TOKENS, HW), jnp.float32, -1.0, 1.0)
    return jnp.clip(joined + jitter, -127.0, 127.0).astype(jnp.bfloat16)


def draw_wo_int(key, part):
    first, second, third = jax.random.split(jax.random.fold_in(key, 5), 3)
    half_width = HW // 2
    base_rows = jax.random.randint(first, (half_width, D), -120, 121)
    errors = jax.random.randint(second, (half_width, D), -6, 7)
    joined = jnp.concatenate([base_rows, errors - base_rows], axis=0).astype(jnp.float32)
    jitter = jax.random.uniform(third, (HW, D), jnp.float32, -1.0, 1.0)
    return jnp.clip(joined + jitter, -127.0, 127.0).astype(jnp.bfloat16)


def draw_gate_int(key, part):
    return int_table(jax.random.fold_in(key, 7), (D, FF_WIN))


def draw_up_int(key, part):
    return int_table(jax.random.fold_in(key, 11), (D, FF_WIN))


def touch_ends(result, stream_key, smallest, high):
    longest = result.shape.index(max(result.shape))
    spots = []
    for shift in (0, 1):
        where = [jax.random.randint(jax.random.fold_in(stream_key, axis), (), 0, length) for axis, length in enumerate(result.shape)]
        where[longest] = (where[longest] + shift) % result.shape[longest]
        spots.append(tuple(where))
    return result.at[spots[0]].set(smallest).at[spots[1]].set(high)


def steps_of(stream_key, extent, cuts, low, high):
    def one(axis_at, blocks):
        steps = jax.random.uniform(jax.random.fold_in(jax.random.fold_in(stream_key, 6), axis_at), (blocks,), jnp.float32, low / len(cuts), high / len(cuts))
        return jnp.repeat(jnp.exp(steps), extent[axis_at] // blocks).reshape((-1,) + (1,) * (len(extent) - axis_at - 1))

    factor_of = one(*cuts[0])
    for cut in cuts[1:]:
        factor_of = factor_of * one(*cut)
    return factor_of


def bell_draw(own_key, dims, spread, reach, cuts=(), held_as=jnp.bfloat16):
    drawn = spread * jax.random.normal(own_key, dims, jnp.float32)
    if cuts:
        drawn = drawn * steps_of(own_key, dims, cuts, -0.22, 0.18)
    return jnp.clip(drawn, -reach, reach).astype(held_as)


def setup_inputs(seed: int = 0, part: int = 0) -> dict:
    key_list = jax.random.split(jax.random.key(seed), 11)
    part_keys = jax.random.split(jax.random.fold_in(key_list[10], part), 11)
    attn_in = draw_attn_in(jax.random.fold_in(jax.random.fold_in(key_list[10], part), 71), part)
    wo_int = draw_wo_int(jax.random.fold_in(key_list[10], 71), part)
    wo_exponent = touch_ends(jax.random.randint(key_list[2], (D,), D_LOG // 3 - 19, D_LOG // 3 - 15), jax.random.fold_in(key_list[2], 1), D_LOG // 3 - 19, (D_LOG // 3 - 15) - 1).astype(jnp.int32)
    token_scale = jnp.clip(jnp.exp(math.log(3.0) - 2.3025851 * jax.random.uniform(part_keys[3], (TOKENS,), jnp.float32) ** steps_of(part_keys[3], (TOKENS,), ((0, 8),), -0.2, 0.2)), 0.3, 3.0)
    residual = bell_draw(part_keys[4], (TOKENS, D), 1.0, 6.0, ((0, 8),))
    norm_gain = jnp.clip(1.0 + 0.1 * jax.random.normal(key_list[5], (D,), jnp.float32), 0.5, 1.5)
    gate_int = draw_gate_int(jax.random.fold_in(key_list[10], 71), part)
    up_int = draw_up_int(jax.random.fold_in(key_list[10], 71), part)
    gate_exponent = touch_ends(jax.random.randint(key_list[8], (FF_WIN,), -8 - D_LOG // 2, -5 - D_LOG // 2), jax.random.fold_in(key_list[8], 1), -8 - D_LOG // 2, (-5 - D_LOG // 2) - 1).astype(jnp.int32)
    up_exponent = touch_ends(jax.random.randint(key_list[9], (FF_WIN,), -8 - D_LOG // 2, -5 - D_LOG // 2), jax.random.fold_in(key_list[9], 1), -8 - D_LOG // 2, (-5 - D_LOG // 2) - 1).astype(jnp.int32)
    return {"attn_in": attn_in, "wo_int": wo_int, "wo_exponent": wo_exponent, "token_scale": token_scale, "residual": residual, "norm_gain": norm_gain, "gate_int": gate_int, "up_int": up_int, "gate_exponent": gate_exponent, "up_exponent": up_exponent}


def normalize(stream, norm_gain):
    widened = stream.astype(jnp.float32)
    inverse = lax.rsqrt(lax.optimization_barrier(jnp.mean(widened * widened, axis=1, keepdims=True)) + 1e-05)
    return (widened * inverse * norm_gain[None, :]).astype(jnp.bfloat16)

def quantize(normed_low):
    widened = lax.optimization_barrier(normed_low).astype(jnp.float32)
    largest = lax.optimization_barrier(jnp.max(jnp.abs(widened), axis=1, keepdims=True))
    xscale = ((largest + 1e-06) / 127.0).astype(jnp.bfloat16)
    levels = jnp.floor(widened / xscale.astype(jnp.float32) + 0.5).astype(jnp.bfloat16)
    return (levels, xscale)

def reference(attn_in, wo_int, wo_exponent, token_scale, residual, norm_gain, gate_int, up_int, gate_exponent, up_exponent):
    proj_int = jnp.dot(attn_in, wo_int, preferred_element_type=jnp.float32)
    col_scale = jnp.exp2(wo_exponent.astype(jnp.float32))
    blocks = proj_int.reshape(N_TENSOR, TOK_DEV, D)
    checksum = lax.optimization_barrier(jnp.sum(blocks, axis=1)) * col_scale[None, :] / TOK_DEV
    attn_out = proj_int * token_scale[:, None] * col_scale[None, :]
    stream = (residual.astype(jnp.float32) + attn_out).astype(jnp.bfloat16)
    levels, xscale = quantize(normalize(stream, norm_gain))
    row_scale = xscale.astype(jnp.float32)
    gate_scale = jnp.exp2(gate_exponent.astype(jnp.float32))[None, :]
    up_scale = jnp.exp2(up_exponent.astype(jnp.float32))[None, :]
    gate_sum = jnp.dot(levels, gate_int, preferred_element_type=jnp.float32) * row_scale * gate_scale
    up_sum = jnp.dot(levels, up_int, preferred_element_type=jnp.float32) * row_scale * up_scale
    hidden = (jax.nn.silu(gate_sum) * up_sum).astype(jnp.bfloat16)
    return (hidden, checksum)
```

```python
import functools

import jax
import jax.numpy as jnp
from jax import lax
from jax.experimental import pallas as pl
from jax.experimental.pallas import tpu as pltpu
from jax.sharding import PartitionSpec as P

MESH = pl.DeviceIdType.MESH
ROWS = 16
EXTRA = 128


def pack(value, dst):
    width = value.shape[1]
    largest = jnp.max(jnp.abs(value), axis=1, keepdims=True)
    exponent = jnp.ceil(jnp.log2(jnp.maximum(largest, 1e-30) * (1.0 / 32000.0)))
    steps = jnp.floor(value * jnp.exp2(-exponent) + 0.5)
    dst[:, :width] = steps.astype(jnp.int32).astype(jnp.int16)
    dst[:, width:] = jnp.broadcast_to(exponent, (value.shape[0], EXTRA)).astype(jnp.int32).astype(jnp.int16)


def unpack(src):
    width = src.shape[1] - EXTRA
    exponent = src[:, width:].astype(jnp.int32).astype(jnp.float32)[:, :1]
    return src[:, :width].astype(jnp.int32).astype(jnp.float32) * jnp.exp2(exponent)


def kernel(
    X, Z, nch,
    attn, wo, wo_exp, token_scale, residual, gain, gate, up, gate_exp, up_exp,
    hidden, checksum,
    wo_v, gate_v, up_v, a_rel, part, keep, xs, xr, zs, zr, total, lev, gate_acc, up_acc,
    wo_sem, weight_sem, xs_sem, xr_sem, zs_sem, zr_sem, gzs_sem, gzr_sem, gxs_sem, gxr_sem,
):
    D = wo.shape[1]
    cw = D // nch
    me = lax.axis_index("tensor")
    z, x = me // X, lax.rem(me, X)
    zrows = Z * ROWS

    def x_peer(d):
        return {"tensor": z * X + lax.rem(x + d, X)}

    def z_peer(d):
        return {"tensor": lax.rem(z + d, Z) * X + x}

    def block_of(d, dz):
        return lax.rem(z + dz, Z) * X + lax.rem(x + d, X)

    def cols(c):
        return pl.ds(pl.multiple_of(c * cw, cw), cw)

    def wo_copy(c):
        return pltpu.make_async_copy(wo.at[:, cols(c)], wo_v.at[:, cols(c)], wo_sem.at[c])

    def remote(src, dst, send, recv, peer):
        return pltpu.make_async_remote_copy(
            src_ref=src, dst_ref=dst, send_sem=send, recv_sem=recv, device_id=peer, device_id_type=MESH
        )

    def x_copy(d, c):
        return remote(xs.at[d - 1, c], xr.at[d - 1, c], xs_sem.at[d - 1, c], xr_sem.at[d - 1, c], x_peer(d))

    def z_copy(d, c):
        return remote(zs.at[d - 1, c], zr.at[d - 1, c], zs_sem.at[d - 1, c], zr_sem.at[d - 1, c], z_peer(d))

    def gz_copy(d, c):
        return remote(
            lev.at[c, pl.ds(0, ROWS)], lev.at[c, pl.ds((Z - d) * ROWS, ROWS)],
            gzs_sem.at[d - 1, c], gzr_sem.at[d - 1, c], z_peer(d),
        )

    def gx_copy(d, c):
        return remote(
            lev.at[c, pl.ds(0, zrows)], lev.at[c, pl.ds((X - d) * zrows, zrows)],
            gxs_sem.at[d - 1, c], gxr_sem.at[d - 1, c], x_peer(d),
        )

    def loop(body):
        lax.fori_loop(0, nch, lambda c, _: (body(c), 0)[1], 0)

    loop(lambda c: wo_copy(c).start())
    gate_copy = pltpu.make_async_copy(gate, gate_v, weight_sem.at[0])
    up_copy = pltpu.make_async_copy(up, up_v, weight_sem.at[1])
    gate_copy.start()
    up_copy.start()

    barrier = pltpu.get_barrier_semaphore()
    for d in range(1, X):
        pl.semaphore_signal(barrier, inc=1, device_id=x_peer(d), device_id_type=MESH)
    for d in range(1, Z):
        pl.semaphore_signal(barrier, inc=1, device_id=z_peer(d), device_id_type=MESH)

    for d in range(X):
        for dz in range(Z):
            a_rel[pl.ds((d * Z + dz) * ROWS, ROWS), :] = attn[
                pl.ds(pl.multiple_of(block_of(d, dz) * ROWS, ROWS), ROWS), :
            ]
    pl.semaphore_wait(barrier, X + Z - 2)

    def project(c):
        wo_copy(c).wait()
        part[...] = jnp.dot(a_rel[...], wo_v[:, cols(c)], preferred_element_type=jnp.float32)
        for d in range(1, X):
            for dz in range(Z):
                pack(part[pl.ds((d * Z + dz) * ROWS, ROWS), :], xs.at[d - 1, c, pl.ds(dz * ROWS, ROWS)])
            x_copy(d, c).start()
        keep[c] = part[:zrows, :]

    loop(project)

    def add_x(c):
        for d in range(1, X):
            x_copy(d, c).wait_recv()
        for step in range(1, Z + 1):
            dz = step % Z
            rows = pl.ds(dz * ROWS, ROWS)
            value = keep[c, rows, :]
            for d in range(1, X):
                value = value + unpack(xr.at[d - 1, c, rows])
            if dz:
                pack(value, zs.at[dz - 1, c])
                z_copy(dz, c).start()
            else:
                total[c] = value

    loop(add_x)

    row_of = lax.broadcasted_iota(jnp.int32, (ROWS, 1), 0)
    row_scale = jnp.zeros((ROWS, 1), jnp.float32)
    for i in range(ROWS):
        row_scale = jnp.where(row_of == i, token_scale[i], row_scale)

    def add_z(c, squares):
        for d in range(1, Z):
            z_copy(d, c).wait_recv()
        value = total[c]
        for d in range(1, Z):
            value = value + unpack(zr.at[d - 1, c])
        col_scale = jnp.exp2(wo_exp[:, cols(c)].astype(jnp.float32))
        checksum[:, cols(c)] = jnp.sum(value, axis=0, keepdims=True) * col_scale / ROWS
        stream = residual[:, cols(c)].astype(jnp.float32) + value * row_scale * col_scale
        stream = stream.astype(jnp.bfloat16).astype(jnp.float32)
        total[c] = stream
        return squares + jnp.sum(stream * stream, axis=1, keepdims=True)

    squares = lax.fori_loop(0, nch, add_z, jnp.zeros((ROWS, 1), jnp.float32))
    inverse = lax.rsqrt(squares / D + 1e-05)

    def norm(c, largest):
        low = (total[c] * inverse * gain[:, cols(c)]).astype(jnp.bfloat16).astype(jnp.float32)
        total[c] = low
        return jnp.maximum(largest, jnp.max(jnp.abs(low), axis=1, keepdims=True))

    largest = lax.fori_loop(0, nch, norm, jnp.zeros((ROWS, 1), jnp.float32))
    xscale = ((largest + 1e-06) / 127.0).astype(jnp.bfloat16)
    xwide = xscale.astype(jnp.float32)

    def send(c):
        lev[c, :ROWS, :cw] = jnp.floor(total[c] / xwide + 0.5).astype(jnp.bfloat16)
        lev[c, :ROWS, cw:] = jnp.broadcast_to(xwide, (ROWS, EXTRA)).astype(jnp.bfloat16)
        for d in range(1, Z):
            gz_copy(d, c).start()

    loop(send)
    gate_acc[...] = jnp.zeros_like(gate_acc)
    up_acc[...] = jnp.zeros_like(up_acc)
    gate_copy.wait()
    up_copy.wait()

    def forward(c):
        for d in range(1, Z):
            gz_copy(d, c).wait_recv()
        for d in range(1, X):
            gx_copy(d, c).start()

    def multiply(c):
        for d in range(1, X):
            gx_copy(d, c).wait_recv()
        levels = lev[c, :, :cw]
        gate_acc[...] += jnp.dot(levels, gate_v[cols(c), :], preferred_element_type=jnp.float32)
        up_acc[...] += jnp.dot(levels, up_v[cols(c), :], preferred_element_type=jnp.float32)

    forward(0)

    def gather(c, _):
        forward(c + 1)
        multiply(c)
        return 0

    lax.fori_loop(0, nch - 1, gather, 0)
    multiply(nch - 1)

    gate_scale = jnp.exp2(gate_exp[...].astype(jnp.float32))
    up_scale = jnp.exp2(up_exp[...].astype(jnp.float32))
    for d in range(X):
        for dz in range(Z):
            rows = pl.ds((d * Z + dz) * ROWS, ROWS)
            scale = lev[0, rows, cw:].astype(jnp.float32)[:, :1]
            g = gate_acc[rows, :] * scale * gate_scale
            u = up_acc[rows, :] * scale * up_scale
            value = g / (1.0 + jnp.exp(-g)) * u
            hidden[pl.ds(pl.multiple_of(block_of(d, dz) * ROWS, ROWS), ROWS), :] = value.astype(jnp.bfloat16)

    def drain(c):
        for d in range(1, X):
            x_copy(d, c).wait_send()
            gx_copy(d, c).wait_send()
        for d in range(1, Z):
            z_copy(d, c).wait_send()
            gz_copy(d, c).wait_send()

    loop(drain)


def local(n, attn_in, wo_int, wo_exponent, token_scale, residual, norm_gain, gate_int, up_int, gate_exponent, up_exponent):
    Z = 4 if n % 4 == 0 else 1
    X = n // Z
    D = wo_int.shape[1]
    nch = 8
    cw = D // nch
    rows, ff = attn_in.shape[0], gate_int.shape[1]
    vmem = pl.BlockSpec(memory_space=pltpu.VMEM)
    anywhere = pl.BlockSpec(memory_space=pl.ANY)
    dma = pltpu.SemaphoreType.DMA
    xn, zn = max(X - 1, 1), max(Z - 1, 1)
    return pl.pallas_call(
        functools.partial(kernel, X, Z, nch),
        out_shape=(
            jax.ShapeDtypeStruct((rows, ff), jnp.bfloat16),
            jax.ShapeDtypeStruct((1, D), jnp.float32),
        ),
        in_specs=[
            vmem, anywhere, vmem, pl.BlockSpec(memory_space=pltpu.SMEM), vmem, vmem, anywhere, anywhere, vmem, vmem,
        ],
        out_specs=(vmem, vmem),
        scratch_shapes=[
            pltpu.VMEM(wo_int.shape, jnp.bfloat16),
            pltpu.VMEM(gate_int.shape, jnp.bfloat16),
            pltpu.VMEM(up_int.shape, jnp.bfloat16),
            pltpu.VMEM(attn_in.shape, jnp.bfloat16),
            pltpu.VMEM((rows, cw), jnp.float32),
            pltpu.VMEM((nch, Z * ROWS, cw), jnp.float32),
            pltpu.VMEM((xn, nch, Z * ROWS, cw + EXTRA), jnp.int16),
            pltpu.VMEM((xn, nch, Z * ROWS, cw + EXTRA), jnp.int16),
            pltpu.VMEM((zn, nch, ROWS, cw + EXTRA), jnp.int16),
            pltpu.VMEM((zn, nch, ROWS, cw + EXTRA), jnp.int16),
            pltpu.VMEM((nch, ROWS, cw), jnp.float32),
            pltpu.VMEM((nch, rows, cw + EXTRA), jnp.bfloat16),
            pltpu.VMEM((rows, ff), jnp.float32),
            pltpu.VMEM((rows, ff), jnp.float32),
            dma((nch,)),
            dma((2,)),
            dma((xn, nch)),
            dma((xn, nch)),
            dma((zn, nch)),
            dma((zn, nch)),
            dma((zn, nch)),
            dma((zn, nch)),
            dma((xn, nch)),
            dma((xn, nch)),
        ],
        compiler_params=pltpu.CompilerParams(
            collective_id=0, has_side_effects=True, vmem_limit_bytes=48 * 1024 * 1024
        ),
        cost_estimate=pl.CostEstimate(
            flops=2 * rows * D * (attn_in.shape[1] + 2 * ff), bytes_accessed=2 * D * (attn_in.shape[1] + 2 * ff),
            transcendentals=rows * ff,
        ),
    )(
        attn_in, wo_int, wo_exponent.reshape(1, D), token_scale, residual, norm_gain.reshape(1, D),
        gate_int, up_int, gate_exponent.reshape(1, ff), up_exponent.reshape(1, ff),
    )


def solution(mesh):
    placed = (
        P("dp", "tensor"),
        P("tensor", None),
        P(),
        P(("dp", "tensor")),
        P(("dp", "tensor"), None),
        P(),
        P(None, "tensor"),
        P(None, "tensor"),
        P("tensor"),
        P("tensor"),
    )
    return jax.shard_map(
        functools.partial(local, mesh.shape["tensor"]),
        mesh=mesh,
        in_specs=placed,
        out_specs=(P("dp", "tensor"), P(("dp", "tensor"), None)),
        check_vma=False,
    )
```

```python
import functools

import jax
import jax.numpy as jnp
from jax import lax
from jax.experimental import pallas as pl
from jax.experimental.pallas import tpu as pltpu
from jax.sharding import PartitionSpec as P

MESH = pl.DeviceIdType.MESH
ROWS = 16
EXTRA = 128


def pack(value, dst):
    width = value.shape[1]
    largest = jnp.max(jnp.abs(value), axis=1, keepdims=True)
    exponent = jnp.ceil(jnp.log2(jnp.maximum(largest, 1e-30) * (1.0 / 32000.0)))
    steps = jnp.floor(value * jnp.exp2(-exponent) + 0.5)
    dst[:, :width] = steps.astype(jnp.int32).astype(jnp.int16)
    dst[:, width:] = jnp.broadcast_to(exponent, (value.shape[0], EXTRA)).astype(jnp.int32).astype(jnp.int16)


def unpack(src):
    width = src.shape[1] - EXTRA
    exponent = src[:, width:].astype(jnp.int32).astype(jnp.float32)[:, :1]
    return src[:, :width].astype(jnp.int32).astype(jnp.float32) * jnp.exp2(exponent)


def kernel(
    X, Z, nch,
    attn_h, wo, wo_exp_h, token_scale_h, residual_h, gain_h, gate, up, gate_exp_h, up_exp_h,
    hidden, checksum,
    attn, wo_exp, token_scale, residual, gain, gate_exp, up_exp,
    wo_v, gate_v, up_v, a_rel, part, keep, xs, xr, zs, zr, total, lev, scales, gate_acc, up_acc,
    small_sem, wo_sem, weight_sem, xs_sem, xr_sem, zs_sem, zr_sem, gs_sem, gr_sem,
):
    D = wo.shape[1]
    cw = D // nch
    me = lax.axis_index("tensor")
    z, x = me // X, lax.rem(me, X)
    zrows = Z * ROWS

    def x_peer(d):
        return {"tensor": z * X + lax.rem(x + d, X)}

    def z_peer(d):
        return {"tensor": lax.rem(z + d, Z) * X + x}

    def block_of(d, dz):
        return lax.rem(z + dz, Z) * X + lax.rem(x + d, X)

    def cols(c):
        return pl.ds(pl.multiple_of(c * cw, cw), cw)

    def wo_copy(c):
        return pltpu.make_async_copy(wo.at[:, cols(c)], wo_v.at[:, cols(c)], wo_sem.at[c])

    def remote(src, dst, send, recv, peer):
        return pltpu.make_async_remote_copy(
            src_ref=src, dst_ref=dst, send_sem=send, recv_sem=recv, device_id=peer, device_id_type=MESH
        )

    def x_copy(d, c):
        return remote(xs.at[d - 1, c], xr.at[d - 1, c], xs_sem.at[d - 1, c], xr_sem.at[d - 1, c], x_peer(d))

    def z_copy(d, c):
        return remote(zs.at[d - 1, c], zr.at[d - 1, c], zs_sem.at[d - 1, c], zr_sem.at[d - 1, c], z_peer(d))

    def place(t, part, c):
        rows = pl.ds(pl.multiple_of(t * ROWS, ROWS), ROWS)
        return lev.at[c, rows] if part == 0 else scales.at[rows]

    def gather_copy(t, part, c, slot, peer):
        ref = place(t, part, c)
        at = c if part == 0 else nch
        return remote(ref, ref, gs_sem.at[slot, at], gr_sem.at[slot, at], peer)

    def right(k, part, c):
        return gather_copy((z - k) * X + x, part, c, k, {"tensor": me + X})

    def left(k, part, c):
        return gather_copy((z + k) * X + x, part, c, Z + k, {"tensor": me - X})

    def across(d, zz, part, c):
        return gather_copy(zz * X + x, part, c, 2 * Z + (d - 1) * Z + zz, x_peer(d))

    def each_part(c, act):
        act(0)
        pl.when(c == 0)(lambda: act(1))

    def start_right(k, c):
        @pl.when(jnp.logical_and(z - k >= 0, z < Z - 1))
        def _():
            each_part(c, lambda part: right(k, part, c).start())

    def start_left(k, c):
        @pl.when(jnp.logical_and(z + k < Z, z > 0))
        def _():
            each_part(c, lambda part: left(k, part, c).start())

    def start_across(zz, c):
        for d in range(1, X):
            each_part(c, lambda part, d=d: across(d, zz, part, c).start())

    def loop(body):
        lax.fori_loop(0, nch, lambda c, _: (body(c), 0)[1], 0)

    small = [
        pltpu.make_async_copy(src, dst, small_sem.at[i])
        for i, (src, dst) in enumerate((
            (attn_h, attn), (wo_exp_h, wo_exp), (token_scale_h, token_scale), (residual_h, residual),
            (gain_h, gain), (gate_exp_h, gate_exp), (up_exp_h, up_exp),
        ))
    ]
    small[0].start()
    loop(lambda c: wo_copy(c).start())
    for copy in small[1:]:
        copy.start()
    gate_copy = pltpu.make_async_copy(gate, gate_v, weight_sem.at[0])
    up_copy = pltpu.make_async_copy(up, up_v, weight_sem.at[1])
    gate_copy.start()
    up_copy.start()

    barrier = pltpu.get_barrier_semaphore()
    for d in range(1, X):
        pl.semaphore_signal(barrier, inc=1, device_id=x_peer(d), device_id_type=MESH)
    for d in range(1, Z):
        pl.semaphore_signal(barrier, inc=1, device_id=z_peer(d), device_id_type=MESH)

    small[0].wait()
    for d in range(X):
        for dz in range(Z):
            a_rel[pl.ds((d * Z + dz) * ROWS, ROWS), :] = attn[
                pl.ds(pl.multiple_of(block_of(d, dz) * ROWS, ROWS), ROWS), :
            ]
    pl.semaphore_wait(barrier, X + Z - 2)

    def project(c):
        wo_copy(c).wait()
        part[...] = jnp.dot(a_rel[...], wo_v[:, cols(c)], preferred_element_type=jnp.float32)
        for d in range(1, X):
            for dz in range(Z):
                pack(part[pl.ds((d * Z + dz) * ROWS, ROWS), :], xs.at[d - 1, c, pl.ds(dz * ROWS, ROWS)])
            x_copy(d, c).start()
        keep[c] = part[:zrows, :]

    loop(project)

    def add_x(c):
        for d in range(1, X):
            x_copy(d, c).wait_recv()
        for step in range(1, Z + 1):
            dz = step % Z
            rows = pl.ds(dz * ROWS, ROWS)
            value = keep[c, rows, :]
            for d in range(1, X):
                value = value + unpack(xr.at[d - 1, c, rows])
            if dz:
                pack(value, zs.at[dz - 1, c])
                z_copy(dz, c).start()
            else:
                total[c] = value

    loop(add_x)

    for copy in small[1:]:
        copy.wait()
    square = (ROWS, ROWS)
    diagonal = lax.broadcasted_iota(jnp.int32, square, 0) == lax.broadcasted_iota(jnp.int32, square, 1)
    spread = jnp.where(diagonal, jnp.broadcast_to(token_scale[...], square), 0.0)
    row_scale = jnp.sum(spread, axis=1, keepdims=True)

    def add_z(c, squares):
        for d in range(1, Z):
            z_copy(d, c).wait_recv()
        value = total[c]
        for d in range(1, Z):
            value = value + unpack(zr.at[d - 1, c])
        col_scale = jnp.exp2(wo_exp[:, cols(c)].astype(jnp.float32))
        checksum[:, cols(c)] = jnp.sum(value, axis=0, keepdims=True) * col_scale / ROWS
        stream = residual[:, cols(c)].astype(jnp.float32) + value * row_scale * col_scale
        stream = stream.astype(jnp.bfloat16).astype(jnp.float32)
        total[c] = stream
        return squares + jnp.sum(stream * stream, axis=1, keepdims=True)

    squares = lax.fori_loop(0, nch, add_z, jnp.zeros((ROWS, 1), jnp.float32))
    inverse = lax.rsqrt(squares / D + 1e-05)

    def norm(c, largest):
        low = (total[c] * inverse * gain[:, cols(c)]).astype(jnp.bfloat16).astype(jnp.float32)
        total[c] = low
        return jnp.maximum(largest, jnp.max(jnp.abs(low), axis=1, keepdims=True))

    largest = lax.fori_loop(0, nch, norm, jnp.zeros((ROWS, 1), jnp.float32))
    xscale = ((largest + 1e-06) / 127.0).astype(jnp.bfloat16)
    xwide = xscale.astype(jnp.float32)

    own_rows = pl.ds(pl.multiple_of(me * ROWS, ROWS), ROWS)
    scales[own_rows, :] = jnp.broadcast_to(xwide, (ROWS, EXTRA)).astype(jnp.bfloat16)

    def send(c):
        lev[c, own_rows, :] = jnp.floor(total[c] / xwide + 0.5).astype(jnp.bfloat16)
        start_right(0, c)
        start_left(0, c)
        start_across(z, c)

    loop(send)
    gate_acc[...] = jnp.zeros_like(gate_acc)
    up_acc[...] = jnp.zeros_like(up_acc)
    gate_copy.wait()
    up_copy.wait()

    def relay(k, c):
        @pl.when(z - 1 - k >= 0)
        def _():
            each_part(c, lambda part: right(k, part, c).wait_recv())
            start_right(k + 1, c)
            start_across(z - 1 - k, c)

        @pl.when(z + 1 + k < Z)
        def _():
            each_part(c, lambda part: left(k, part, c).wait_recv())
            start_left(k + 1, c)
            start_across(z + 1 + k, c)

    def multiply(c):
        for d in range(1, X):
            for zz in range(Z):
                each_part(c, lambda part, d=d, zz=zz: across(d, zz, part, c).wait_recv())
        levels = lev[c]
        gate_acc[...] += jnp.dot(levels, gate_v[cols(c), :], preferred_element_type=jnp.float32)
        up_acc[...] += jnp.dot(levels, up_v[cols(c), :], preferred_element_type=jnp.float32)

    def gather(step, _):
        for k in range(Z - 1):
            c = step - k

            @pl.when(jnp.logical_and(c >= 0, c < nch))
            def _(k=k, c=c):
                relay(k, c)

        @pl.when(step >= Z)
        def _():
            multiply(step - Z)

        return 0

    lax.fori_loop(0, nch + Z, gather, 0)

    gate_scale = jnp.exp2(gate_exp[...].astype(jnp.float32))
    up_scale = jnp.exp2(up_exp[...].astype(jnp.float32))
    for t in range(X * Z):
        rows = pl.ds(t * ROWS, ROWS)
        scale = scales[rows, :].astype(jnp.float32)[:, :1]
        g = gate_acc[rows, :] * scale * gate_scale
        u = up_acc[rows, :] * scale * up_scale
        hidden[rows, :] = (g / (1.0 + jnp.exp(-g)) * u).astype(jnp.bfloat16)

    def drain(c):
        for d in range(1, X):
            x_copy(d, c).wait_send()
            for zz in range(Z):
                each_part(c, lambda part, d=d, zz=zz: across(d, zz, part, c).wait_send())
        for d in range(1, Z):
            z_copy(d, c).wait_send()
        for k in range(Z):
            @pl.when(jnp.logical_and(z - k >= 0, z < Z - 1))
            def _(k=k):
                each_part(c, lambda part: right(k, part, c).wait_send())

            @pl.when(jnp.logical_and(z + k < Z, z > 0))
            def _(k=k):
                each_part(c, lambda part: left(k, part, c).wait_send())

    loop(drain)


def local(n, attn_in, wo_int, wo_exponent, token_scale, residual, norm_gain, gate_int, up_int, gate_exponent, up_exponent):
    Z = 4 if n % 4 == 0 else 1
    X = n // Z
    D = wo_int.shape[1]
    nch = 8
    cw = D // nch
    rows, ff = attn_in.shape[0], gate_int.shape[1]
    vmem = pl.BlockSpec(memory_space=pltpu.VMEM)
    anywhere = pl.BlockSpec(memory_space=pl.ANY)
    dma = pltpu.SemaphoreType.DMA
    xn, zn = max(X - 1, 1), max(Z - 1, 1)
    return pl.pallas_call(
        functools.partial(kernel, X, Z, nch),
        out_shape=(
            jax.ShapeDtypeStruct((rows, ff), jnp.bfloat16),
            jax.ShapeDtypeStruct((1, D), jnp.float32),
        ),
        in_specs=[anywhere] * 10,
        out_specs=(vmem, vmem),
        scratch_shapes=[
            pltpu.VMEM(attn_in.shape, jnp.bfloat16),
            pltpu.VMEM((1, D), jnp.int32),
            pltpu.VMEM((1, ROWS), jnp.float32),
            pltpu.VMEM(residual.shape, jnp.bfloat16),
            pltpu.VMEM((1, D), jnp.float32),
            pltpu.VMEM((1, ff), jnp.int32),
            pltpu.VMEM((1, ff), jnp.int32),
            pltpu.VMEM(wo_int.shape, jnp.bfloat16),
            pltpu.VMEM(gate_int.shape, jnp.bfloat16),
            pltpu.VMEM(up_int.shape, jnp.bfloat16),
            pltpu.VMEM(attn_in.shape, jnp.bfloat16),
            pltpu.VMEM((rows, cw), jnp.float32),
            pltpu.VMEM((nch, Z * ROWS, cw), jnp.float32),
            pltpu.VMEM((xn, nch, Z * ROWS, cw + EXTRA), jnp.int16),
            pltpu.VMEM((xn, nch, Z * ROWS, cw + EXTRA), jnp.int16),
            pltpu.VMEM((zn, nch, ROWS, cw + EXTRA), jnp.int16),
            pltpu.VMEM((zn, nch, ROWS, cw + EXTRA), jnp.int16),
            pltpu.VMEM((nch, ROWS, cw), jnp.float32),
            pltpu.VMEM((nch, rows, cw), jnp.bfloat16),
            pltpu.VMEM((rows, EXTRA), jnp.bfloat16),
            pltpu.VMEM((rows, ff), jnp.float32),
            pltpu.VMEM((rows, ff), jnp.float32),
            dma((7,)),
            dma((nch,)),
            dma((2,)),
            dma((xn, nch)),
            dma((xn, nch)),
            dma((zn, nch)),
            dma((zn, nch)),
            dma((2 * Z + xn * Z, nch + 1)),
            dma((2 * Z + xn * Z, nch + 1)),
        ],
        compiler_params=pltpu.CompilerParams(
            collective_id=0, has_side_effects=True, vmem_limit_bytes=60 * 1024 * 1024
        ),
        cost_estimate=pl.CostEstimate(
            flops=2 * rows * D * (attn_in.shape[1] + 2 * ff), bytes_accessed=2 * D * (attn_in.shape[1] + 2 * ff),
            transcendentals=rows * ff,
        ),
    )(
        attn_in, wo_int, wo_exponent.reshape(1, D), token_scale.reshape(1, ROWS), residual, norm_gain.reshape(1, D),
        gate_int, up_int, gate_exponent.reshape(1, ff), up_exponent.reshape(1, ff),
    )


def solution(mesh):
    placed = (
        P("dp", "tensor"),
        P("tensor", None),
        P(),
        P(("dp", "tensor")),
        P(("dp", "tensor"), None),
        P(),
        P(None, "tensor"),
        P(None, "tensor"),
        P("tensor"),
        P("tensor"),
    )
    return jax.shard_map(
        functools.partial(local, mesh.shape["tensor"]),
        mesh=mesh,
        in_specs=placed,
        out_specs=(P("dp", "tensor"), P(("dp", "tensor"), None)),
        check_vma=False,
    )
```
